256 devices in a mesh: tm: 64 (over y_lo, x, z), rows: 4 (over y_hi, core).
Axes of the slice: x: 4, y: 4 (y_hi: 2, y_lo: 2; y = y_hi * 2 + y_lo), z: 8, core: 2. Of those that a mesh axis runs over, the one named last changes fastest.
Arguments:
- latents: bfloat16 [128, 24, 24, 1280], P('tm', 'rows'), may hold values from -40 to 40
- reference_features: bfloat16 [4608, 1280], P(('tm', 'rows')), may hold values from -12 to 12
- norm_gain: float32 [1280], replicated, may hold values from 0.2 to 5
- query_weight: bfloat16 [1280, 640], replicated, may hold values from -3 to 3
- key_weight: bfloat16 [1280, 640], replicated, may hold values from -3 to 3
- value_weight: bfloat16 [1280, 640], replicated, may hold values from -0.15625 to 0.15625
- out_weight: bfloat16 [640, 1280], replicated, may hold values from -1 to 1
- out_bias: float32 [1280], replicated, may hold values from -3 to 3
- motion_gain: float32 [1280], replicated, may hold values from 0.1 to 1.9
- motion_query: bfloat16 [1280, 640], replicated, may hold values from -3 to 3
- motion_key: bfloat16 [1280, 640], replicated, may hold values from -3 to 3
- motion_value: bfloat16 [1280, 640], replicated, may hold values from -0.15625 to 0.15625
Outputs:
- block_out: bfloat16 [128, 24, 24, 1280], P('tm', 'rows')
- motion_heads: bfloat16 [128, 24, 24, 640], P('tm', 'rows')
The draws below stay inside these ranges and needn't reach their ends.
All inputs are finite; a program needn't handle non-finite values.
Results may differ from the reference program's by a relative error of at most 0.018.
Values may be sent and summed in bfloat16 or wider, within the bound.
No kernel may reach another device: no remote copies, remote signals or barrier semaphores. Data moves between devices by JAX's collectives and lax.ppermute only.
A program may use at most 128 MiB of HBM per device.

```python
import math
import jax
import jax.numpy as jnp
from jax import lax

D = 1280
GROUPS = 32
HEADS = 4
HD = 160
THEADS = 4
THD = 160
GRID = 24
SHOT = 16
FRAMES = 128
SHOTS = 8


def drawn_weight(key, columns):
    return jax.random.truncated_normal(key, -4.0, 4.0, (D, columns), jnp.float32) / math.sqrt(D)


def draw_latents(key, part):
    key = jax.random.fold_in(key, 11)
    key_noise, key_chan = jax.random.split(key, 2)
    noise = jax.random.truncated_normal(key_noise, -4.0, 4.0, (FRAMES, GRID, GRID, D), jnp.float32)
    row_scale = 0.5 + jnp.arange(GRID, dtype=jnp.float32) / max(GRID - 1, 1)
    chan_scale = jnp.exp(jax.random.uniform(key_chan, (D,), jnp.float32, -0.7, 0.7))
    return (noise * row_scale[None, :, None, None] * chan_scale).astype(jnp.bfloat16)


def draw_query_weight(key, part):
    key = jax.random.fold_in(key, 21)
    weights = drawn_weight(key, HEADS * HD)
    return weights.astype(jnp.bfloat16)


def draw_key_weight(key, part):
    key = jax.random.fold_in(key, 22)
    weights = drawn_weight(key, HEADS * HD)
    return weights.astype(jnp.bfloat16)


def draw_motion_query(key, part):
    key = jax.random.fold_in(key, 23)
    weights = drawn_weight(key, THEADS * THD)
    return weights.astype(jnp.bfloat16)


def draw_motion_key(key, part):
    key = jax.random.fold_in(key, 24)
    weights = drawn_weight(key, THEADS * THD)
    return weights.astype(jnp.bfloat16)


def level_of(rng, extent, cuts, least, top_value):
    gain = 1.0
    for dim, shards_of in cuts:
        steps = jax.random.uniform(jax.random.fold_in(jax.random.fold_in(rng, 6), dim), (shards_of,), jnp.float32, least / len(cuts), top_value / len(cuts))
        gain = gain * jnp.repeat(jnp.exp(steps), extent[dim] // shards_of).reshape((-1,) + (1,) * (len(extent) - 1 - dim))
    return gain


def gaussian(own_key, extent, scale, bound, shards=(), held_as=jnp.bfloat16):
    entries = jax.random.normal(own_key, extent, jnp.float32) * scale
    if len(shards) > 0:
        entries = level_of(own_key, extent, shards, -0.22, 0.18) * entries
    return jnp.clip(entries, min=-bound, max=bound).astype(held_as)


def setup_inputs(seed: int = 0) -> dict:
    splits = jax.random.split(jax.random.key(seed), 13)
    latents = draw_latents(jax.random.fold_in(splits[12], 71), 0)
    reference_features = gaussian(splits[1], (SHOTS * GRID * GRID, D), 3.0, 12.0, ((0, 256),))
    norm_gain = jnp.clip(jnp.exp(jax.random.uniform(splits[2], (D,), jnp.float32, math.log(0.2), math.log(5.0))), 0.2, 5.0)
    query_weight = draw_query_weight(jax.random.fold_in(splits[12], 71), 0)
    key_weight = draw_key_weight(jax.random.fold_in(splits[12], 71), 0)
    value_weight = gaussian(splits[5], (D, HEADS * HD), D ** -0.5, 0.15625)
    out_weight = gaussian(splits[6], (HEADS * HD, D), (HEADS * HD // 16) ** -0.5, 1.0)
    out_bias = gaussian(splits[7], (D,), 0.5, 3.0, (), jnp.float32)
    motion_gain = jnp.clip(1.0 + 0.18 * jax.random.normal(splits[8], (D,), jnp.float32), 0.1, 1.9)
    motion_query = draw_motion_query(jax.random.fold_in(splits[12], 71), 0)
    motion_key = draw_motion_key(jax.random.fold_in(splits[12], 71), 0)
    motion_value = gaussian(splits[11], (D, THEADS * THD), D ** -0.5, 0.15625)
    return {"latents": latents, "reference_features": reference_features, "norm_gain": norm_gain, "query_weight": query_weight, "key_weight": key_weight, "value_weight": value_weight, "out_weight": out_weight, "out_bias": out_bias, "motion_gain": motion_gain, "motion_query": motion_query, "motion_key": motion_key, "motion_value": motion_value}


def position_codes(positions, channels):
    halves = jnp.arange(channels // 2, dtype=jnp.float32)
    rates = jnp.exp(-math.log(10000.0) * 2.0 * halves / channels)
    angles = positions[:, None] * rates[None, :]
    return jnp.stack([jnp.sin(angles), jnp.cos(angles)], axis=-1).reshape(positions.shape[0], channels)

def spatial_frame(query_rows, key_rows, value_rows, ref_key_rows, ref_value_rows):
    all_keys = jnp.concatenate([key_rows, ref_key_rows], axis=0).astype(jnp.float32)
    all_values = jnp.concatenate([value_rows, ref_value_rows], axis=0).astype(jnp.float32)
    scores = jnp.einsum('phd,khd->hpk', query_rows.astype(jnp.float32), all_keys) / math.sqrt(HD)
    highest = lax.optimization_barrier(jnp.max(scores, axis=-1, keepdims=True))
    exps = jnp.exp(scores - highest)
    totals = lax.optimization_barrier(jnp.sum(exps, axis=-1))
    weights = exps.astype(jnp.bfloat16).astype(jnp.float32)
    mixed = jnp.einsum('hpk,khd->phd', weights, all_values) / jnp.transpose(totals)[:, :, None]
    return mixed.astype(jnp.bfloat16).reshape(query_rows.shape[0], HEADS * HD)

def frame_attention(motion_q, motion_k, motion_v):
    query_count, cells = (motion_q.shape[0], motion_q.shape[1])
    query_heads = motion_q.reshape(query_count, cells, THEADS, THD).astype(jnp.float32)
    key_heads = motion_k.reshape(motion_k.shape[0], cells, THEADS, THD).astype(jnp.float32)
    value_heads = motion_v.reshape(motion_v.shape[0], cells, THEADS, THD).astype(jnp.float32)
    scores = jnp.einsum('fphd,gphd->phfg', query_heads, key_heads) / math.sqrt(THD)
    highest = lax.optimization_barrier(jnp.max(scores, axis=-1, keepdims=True))
    exps = jnp.exp(scores - highest)
    totals = lax.optimization_barrier(jnp.sum(exps, axis=-1))
    weights = exps.astype(jnp.bfloat16).astype(jnp.float32)
    mixed = jnp.einsum('phfg,gphd->fphd', weights, value_heads) / jnp.transpose(totals, (2, 0, 1))[..., None]
    return mixed.astype(jnp.bfloat16).reshape(query_count, cells, THEADS * THD)

def reference(latents, reference_features, norm_gain, query_weight, key_weight, value_weight, out_weight, out_bias, motion_gain, motion_query, motion_key, motion_value):
    places = GRID * GRID
    grouped = latents.astype(jnp.float32).reshape(FRAMES, places, GROUPS, D // GROUPS)
    group_mean = lax.optimization_barrier(jnp.mean(grouped, axis=(1, 3)))
    group_square = lax.optimization_barrier(jnp.mean(grouped * grouped, axis=(1, 3)))
    group_var = group_square - group_mean * group_mean
    normed = (grouped - group_mean[:, None, :, None]) * lax.rsqrt(group_var + 1e-05)[:, None, :, None]
    normed = (normed.reshape(FRAMES, places, D) * norm_gain).astype(jnp.bfloat16)
    flat_normed = normed.reshape(FRAMES * places, D)
    queries = jnp.dot(flat_normed, query_weight, preferred_element_type=jnp.float32).astype(jnp.bfloat16)
    keys = jnp.dot(flat_normed, key_weight, preferred_element_type=jnp.float32).astype(jnp.bfloat16)
    values = jnp.dot(flat_normed, value_weight, preferred_element_type=jnp.float32).astype(jnp.bfloat16)
    queries = queries.reshape(SHOTS, SHOT, places, HEADS, HD)
    keys = keys.reshape(SHOTS, SHOT, places, HEADS, HD)
    values = values.reshape(SHOTS, SHOT, places, HEADS, HD)
    ref_keys = jnp.dot(reference_features, key_weight, preferred_element_type=jnp.float32).astype(jnp.bfloat16)
    ref_values = jnp.dot(reference_features, value_weight, preferred_element_type=jnp.float32).astype(jnp.bfloat16)
    ref_keys = ref_keys.reshape(SHOTS, places, HEADS, HD)
    ref_values = ref_values.reshape(SHOTS, places, HEADS, HD)

    def one_shot(pieces):
        shot_q, shot_k, shot_v, shot_rk, shot_rv = pieces
        return lax.map(lambda trio: spatial_frame(trio[0], trio[1], trio[2], shot_rk, shot_rv), (shot_q, shot_k, shot_v))
    attended = lax.map(one_shot, (queries, keys, values, ref_keys, ref_values))
    attended = attended.reshape(FRAMES * places, HEADS * HD)
    block = latents.astype(jnp.float32).reshape(FRAMES * places, D) + jnp.dot(attended, out_weight, preferred_element_type=jnp.float32) + out_bias
    block_out = block.astype(jnp.bfloat16)
    block_wide = block_out.astype(jnp.float32).reshape(FRAMES, places, D)
    cell_mean = lax.optimization_barrier(jnp.mean(block_wide, axis=-1, keepdims=True))
    centered = block_wide - cell_mean
    cell_var = lax.optimization_barrier(jnp.mean(centered * centered, axis=-1, keepdims=True))
    frame_pos = (jnp.arange(FRAMES, dtype=jnp.int32) % SHOT).astype(jnp.float32)
    codes = position_codes(frame_pos, D)
    motion_in = (centered * lax.rsqrt(cell_var + 1e-05) * motion_gain + codes[:, None, :]).astype(jnp.bfloat16)
    motion_flat = motion_in.reshape(FRAMES * places, D)
    motion_q = jnp.dot(motion_flat, motion_query, preferred_element_type=jnp.float32).astype(jnp.bfloat16)
    motion_k = jnp.dot(motion_flat, motion_key, preferred_element_type=jnp.float32).astype(jnp.bfloat16)
    motion_v = jnp.dot(motion_flat, motion_value, preferred_element_type=jnp.float32).astype(jnp.bfloat16)
    motion_q = motion_q.reshape(SHOTS, SHOT, places, THEADS * THD)
    motion_k = motion_k.reshape(SHOTS, SHOT, places, THEADS * THD)
    motion_v = motion_v.reshape(SHOTS, SHOT, places, THEADS * THD)
    motion_heads = lax.map(lambda trio: frame_attention(trio[0], trio[1], trio[2]), (motion_q, motion_k, motion_v))
    return (block_out.reshape(FRAMES, GRID, GRID, D), motion_heads.reshape(FRAMES, GRID, GRID, THEADS * THD))
```

```python
import functools
import math

import jax
import jax.numpy as jnp
import numpy as np
from jax import lax
from jax.experimental import pallas as pl
from jax.experimental.pallas import tpu as pltpu
from jax.sharding import PartitionSpec as P

GROUPS = 32
HEADS = 4
HD = 160
SHOT = 16
WINDOWS = tuple(HD * h // 128 * 128 for h in range(HEADS))
SCALE = math.log2(math.e) / math.sqrt(HD)
AXES = ("tm", "rows")
MAIN = 16
NT = (((1,), (1,)), ((), ()))
VMEM = 40 * 1024 * 1024


def mesh_perm(move):
    def flat(yl, x, z, yh, c):
        return ((yl * 4 + x) * 8 + z) * 4 + yh * 2 + c

    places = [
        (yl, x, z, yh, c)
        for yl in range(2)
        for x in range(4)
        for z in range(8)
        for yh in range(2)
        for c in range(2)
    ]
    return [(flat(*p), flat(*move(*p))) for p in places]


Y_FLIP = mesh_perm(lambda yl, x, z, yh, c: (yl, x, z, 1 - yh, c))
C_FLIP = mesh_perm(lambda yl, x, z, yh, c: (yl, x, z, yh, 1 - c))
YC_FLIP = mesh_perm(lambda yl, x, z, yh, c: (yl, x, z, 1 - yh, 1 - c))
Z_RING = mesh_perm(lambda yl, x, z, yh, c: (yl, x, (z + (1 if c == 0 else 7)) % 8, yh, c))


def send(value, pairs):
    return lax.ppermute(value, AXES, pairs)


def shot_groups():
    return [list(range(8 * g, 8 * g + 8)) for g in range(8)]


def exchange(value):
    return lax.all_to_all(value, "tm", 0, 0, axis_index_groups=shot_groups(), tiled=True)


def position_codes(channels):
    halves = np.arange(channels // 2, dtype=np.float64)
    rates = np.exp(-math.log(10000.0) * 2.0 * halves / channels)
    angles = np.arange(SHOT, dtype=np.float64)[:, None] * rates[None, :]
    return np.stack([np.sin(angles), np.cos(angles)], axis=-1).reshape(SHOT, channels).astype(
        np.float32
    )


def call(kernel, out_shape, args, in_specs=None, scratch=(), flops=0, moved=0):
    return pl.pallas_call(
        kernel,
        out_shape=out_shape,
        grid=(1,),
        in_specs=in_specs or [whole(a) for a in args],
        out_specs=jax.tree.map(whole, out_shape),
        scratch_shapes=scratch,
        compiler_params=pltpu.CompilerParams(vmem_limit_bytes=VMEM),
        cost_estimate=pl.CostEstimate(flops=flops, bytes_accessed=moved, transcendentals=0),
    )(*args)


def whole(a):
    rank = len(a.shape)
    return pl.BlockSpec(a.shape, lambda i: (0,) * rank)


def head_window(x, h):
    w = WINDOWS[h]
    part = x[:, w : w + 256]
    lane = lax.broadcasted_iota(jnp.int32, part.shape, 1)
    low = HD * h - w
    return jnp.where((lane >= low) & (lane < low + HD), part, jnp.zeros_like(part))


def side_by_side(parts):
    lane = lax.broadcasted_iota(jnp.int32, (parts[0].shape[0], 128), 1)
    cols = [parts[0][:, :128]]
    for h in range(1, HEADS):
        edge = HD * h - WINDOWS[h]
        cols.append(jnp.where(lane < edge, parts[h - 1][:, 128:], parts[h][:, :128]))
    cols.append(parts[HEADS - 1][:, 128:])
    return jnp.concatenate(cols, axis=1)


def dot(a, b):
    return jnp.dot(a, b, preferred_element_type=jnp.float32)


def group_stats(s1, s2, count):
    channels = s1.shape[1]
    width = channels // GROUPS
    ch = lax.broadcasted_iota(jnp.int32, (channels, 128), 0)
    gr = lax.broadcasted_iota(jnp.int32, (channels, 128), 1) * width
    member = jnp.where((ch >= gr) & (ch < gr + width), 1.0, 0.0)
    row = lax.broadcasted_iota(jnp.int32, (8, channels), 0)
    both = jnp.where(row == 0, s1, jnp.where(row == 1, s2, 0.0))
    sums = jnp.dot(both, member, precision=lax.Precision.HIGHEST) / count
    mean, square = sums[0:1], sums[1:2]
    rstd = lax.rsqrt(square - mean * mean + 1e-05)
    row = lax.broadcasted_iota(jnp.int32, (8, 128), 0)
    both = jnp.where(row == 0, mean, jnp.where(row == 1, rstd, 0.0))
    spread = lax.dot_general(both, member, NT, precision=lax.Precision.HIGHEST)
    return spread[0:1], spread[1:2]


def own_kernel(own, peer_c, peer_y, peer_yc, gain, wq, wk, wv, q_out, o_out, ml_out, xn, k, v):
    pieces = (own, peer_c, peer_y, peer_yc)
    places, channels = own.shape
    s1 = jnp.zeros((1, channels), jnp.float32)
    s2 = jnp.zeros((1, channels), jnp.float32)
    for piece in pieces:
        x = piece[...].astype(jnp.float32)
        s1 += jnp.sum(x, axis=0, keepdims=True)
        s2 += jnp.sum(x * x, axis=0, keepdims=True)
    mean, rstd = group_stats(s1, s2, 4 * places * (channels // GROUPS))
    for i, piece in enumerate(pieces):
        x = piece[...].astype(jnp.float32)
        xn[i * places : (i + 1) * places, :] = ((x - mean) * rstd * gain[...]).astype(jnp.bfloat16)
    q = dot(xn[:places, :], wq[...]).astype(jnp.bfloat16)
    q_out[...] = q
    k[...] = dot(xn[...], wk[...]).astype(jnp.bfloat16)
    v[...] = dot(xn[...], wv[...]).astype(jnp.bfloat16)
    lane = lax.broadcasted_iota(jnp.int32, (places, 128), 1)
    ml = jnp.zeros((places, 128), jnp.float32)
    for h in range(HEADS):
        w = WINDOWS[h]
        s = lax.dot_general(
            head_window(q, h), k[:, w : w + 256], NT, preferred_element_type=jnp.float32
        )
        top = jnp.max(s, axis=1, keepdims=True)
        p = jnp.exp2((s - top) * SCALE)
        total = jnp.sum(p, axis=1, keepdims=True)
        o_out[h] = dot(p.astype(jnp.bfloat16), v[:, w : w + 256])
        ml = jnp.where(lane == h, top, jnp.where(lane == HEADS + h, total, ml))
    ml_out[...] = ml


def ref_kernel(t0, t1, t2, t3, t4, t5, t6, t7, wk, wv, k_out, v_out):
    x = jnp.concatenate([t[...] for t in (t0, t1, t2, t3, t4, t5, t6, t7)], axis=0)
    k_out[...] = dot(x, wk[...]).astype(jnp.bfloat16)
    v_out[...] = dot(x, wv[...]).astype(jnp.bfloat16)


def join_kernel(q0, o0, ml0, q1, o1, ml1, rk, rv, att_out, packed, tail):
    places = q0.shape[0]
    for f, (q, o, ml) in enumerate(((q0, o0, ml0), (q1, o1, ml1))):
        parts = []
        for h in range(HEADS):
            w = WINDOWS[h]
            s = lax.dot_general(
                head_window(q[...], h), rk[:, w : w + 256], NT, preferred_element_type=jnp.float32
            )
            before = ml[:, h : h + 1]
            top = jnp.maximum(before, jnp.max(s, axis=1, keepdims=True))
            p = jnp.exp2((s - top) * SCALE)
            keep = jnp.exp2((before - top) * SCALE)
            total = ml[:, HEADS + h : HEADS + h + 1] * keep + jnp.sum(p, axis=1, keepdims=True)
            mixed = o[h] * keep + dot(p.astype(jnp.bfloat16), rv[:, w : w + 256])
            parts.append(mixed / total)
        att = side_by_side(parts)
        att_out[f] = att.astype(jnp.bfloat16)
        for d in range(8):
            packed[d, MAIN * f : MAIN * f + MAIN, :] = att_out[f, MAIN * d : MAIN * d + MAIN, :]
        tail[f] = att[8 * MAIN :, :]
    pack_tail(tail, packed, 2 * MAIN)


def pack_tail(tail, packed, base):
    width = tail.shape[2]
    for d in range(8):
        rows = [tail[f, 2 * d : 2 * d + 2, :] for f in range(2)]
        rows.append(jnp.zeros((4, width), jnp.float32))
        packed[d, base : base + 8, :] = jnp.concatenate(rows, axis=0).astype(jnp.bfloat16)


def pack_kernel(lat, packed, tail):
    half = lat.shape[2] // 2
    for f in range(2):
        for s in range(2):
            for d in range(8):
                at = 2 * MAIN * s + MAIN * f
                packed[d, at : at + MAIN, :] = lat[
                    f, MAIN * d : MAIN * d + MAIN, half * s : half * s + half
                ]
        tail[f] = lat[f, 8 * MAIN :, :].astype(jnp.float32)
    for d in range(8):
        rows = [
            tail[f, 2 * d : 2 * d + 2, half * s : half * s + half]
            for s in range(2)
            for f in range(2)
        ]
        packed[d, 4 * MAIN : 4 * MAIN + 8, :] = jnp.concatenate(rows, axis=0).astype(jnp.bfloat16)


def block_kernel(lat, att, wo, bias, out):
    for f in range(2):
        out[f] = (
            lat[f].astype(jnp.float32) + dot(att[f], wo[...]) + bias[...]
        ).astype(jnp.bfloat16)


def layer_norm(x, gain, codes):
    mean = jnp.mean(x, axis=-1, keepdims=True)
    centered = x - mean
    var = jnp.mean(centered * centered, axis=-1, keepdims=True)
    return centered * lax.rsqrt(var + 1e-05) * gain + codes


def masked_attention(q, k, v, same):
    parts = []
    for h in range(HEADS):
        w = WINDOWS[h]
        s = lax.dot_general(
            head_window(q, h), k[:, w : w + 256], NT, preferred_element_type=jnp.float32
        )
        s = jnp.where(same, s, -jnp.inf)
        top = jnp.max(s, axis=1, keepdims=True)
        p = jnp.exp2((s - top) * SCALE)
        total = jnp.sum(p, axis=1, keepdims=True)
        parts.append(dot(p.astype(jnp.bfloat16), v[:, w : w + 256]) / total)
    return side_by_side(parts)


def motion_kernel(
    lat, att, wo, bias, gain, codes, tail_codes, wq, wk, wv, out, x, q, k, v
):
    half = lat.shape[2]
    channels = 2 * half
    main_rows = 8 * 2 * MAIN
    tail_rows = 64
    main_att = att[:, : 2 * MAIN, :].reshape(main_rows, half)
    tail_att = att[:, 2 * MAIN :, :].reshape(tail_rows, half)
    main_left = lat[:, : 2 * MAIN, :].reshape(main_rows, half).astype(jnp.float32)
    main_right = lat[:, 2 * MAIN : 4 * MAIN, :].reshape(main_rows, half).astype(jnp.float32)
    tail_left = lat[:, 4 * MAIN :, :].reshape(tail_rows, half).astype(jnp.float32)
    tail_right = pltpu.roll(tail_left, tail_rows - 4, 0)
    main = jnp.concatenate([main_left, main_right], axis=1) + dot(main_att, wo[...]) + bias[...]
    main = main.astype(jnp.bfloat16).astype(jnp.float32)
    code_rows = jnp.broadcast_to(codes[...][:, None, :], (SHOT, MAIN, channels))
    x[:main_rows, :] = layer_norm(
        main, gain[...], code_rows.reshape(main_rows, channels)
    ).astype(jnp.bfloat16)
    tail = jnp.concatenate([tail_left, tail_right], axis=1) + dot(tail_att, wo[...]) + bias[...]
    tail = tail.astype(jnp.bfloat16).astype(jnp.float32)
    x[main_rows:, :] = layer_norm(tail, gain[...], tail_codes[...]).astype(jnp.bfloat16)
    q[...] = dot(x[...], wq[...]).astype(jnp.bfloat16)
    k[...] = dot(x[...], wk[...]).astype(jnp.bfloat16)
    v[...] = dot(x[...], wv[...]).astype(jnp.bfloat16)
    row = lax.broadcasted_iota(jnp.int32, (main_rows, main_rows), 0)
    col = lax.broadcasted_iota(jnp.int32, (main_rows, main_rows), 1)
    heads = masked_attention(
        q[:main_rows, :], k[:main_rows, :], v[:main_rows, :], (row & 15) == (col & 15)
    ).astype(jnp.bfloat16)
    out[:, : 2 * MAIN, :] = heads.reshape(8, 2 * MAIN, half)
    row = lax.broadcasted_iota(jnp.int32, (tail_rows, tail_rows), 0)
    col = lax.broadcasted_iota(jnp.int32, (tail_rows, tail_rows), 1)
    heads = masked_attention(
        q[main_rows:, :], k[main_rows:, :], v[main_rows:, :], ((row ^ col) & 5) == 0
    ).astype(jnp.bfloat16)
    out[:, 2 * MAIN :, :] = heads.reshape(8, 8, half)


def place_kernel(packed, out, tail):
    for d in range(8):
        for f in range(2):
            out[f, MAIN * d : MAIN * d + MAIN, :] = packed[d, MAIN * f : MAIN * f + MAIN, :]
        rest = packed[d, 2 * MAIN :, :].astype(jnp.float32)
        for f in range(2):
            tail[f, 2 * d : 2 * d + 2, :] = rest[2 * f : 2 * f + 2, :]
    for f in range(2):
        out[f, 8 * MAIN :, :] = tail[f].astype(jnp.bfloat16)


def body(
    latents,
    reference_features,
    norm_gain,
    query_weight,
    key_weight,
    value_weight,
    out_weight,
    out_bias,
    motion_gain,
    motion_query,
    motion_key,
    motion_value,
):
    frames, row_count, col_count, channels = latents.shape
    places = row_count * col_count
    width = query_weight.shape[1]
    bf16 = functools.partial(jax.ShapeDtypeStruct, dtype=jnp.bfloat16)
    f32 = functools.partial(jax.ShapeDtypeStruct, dtype=jnp.float32)
    lat = latents.reshape(frames, places, channels)
    gain = norm_gain.reshape(1, channels)
    bias = out_bias.reshape(1, channels)
    motion = motion_gain.reshape(1, channels)

    from_y = [send(lat[f], Y_FLIP) for f in range(2)]
    from_c = send(lat, C_FLIP)
    from_yc = [send(from_y[f], C_FLIP) for f in range(2)]

    own = reference_features
    tokens = jnp.concatenate(
        [own] + [send(own, pairs) for pairs in (C_FLIP, Y_FLIP, YC_FLIP)], axis=0
    )
    ring = [tokens]
    for _ in range(4):
        ring.append(send(ring[-1], Z_RING))
    other = send(jnp.stack(ring[1:4]), C_FLIP)
    token_parts = ring + [other[0], other[1], other[2]]

    packed_lat = call(
        pack_kernel,
        bf16((8, 72, width)),
        (lat,),
        scratch=[pltpu.VMEM((2, 16, channels), jnp.float32)],
        moved=1500000,
    )
    lat_cells = exchange(packed_lat)

    own_parts = []
    for f in range(2):
        pick = pl.BlockSpec((None, places, channels), lambda i, f=f: (f, 0, 0))
        args = (lat, from_c, from_y[f], from_yc[f], gain, query_weight, key_weight, value_weight)
        own_parts.append(
            call(
                own_kernel,
                (
                    bf16((places, width)),
                    f32((HEADS, places, 256)),
                    f32((places, 128)),
                ),
                args,
                in_specs=[pick, pick] + [whole(a) for a in args[2:]],
                scratch=[
                    pltpu.VMEM((4 * places, channels), jnp.bfloat16),
                    pltpu.VMEM((4 * places, width), jnp.bfloat16),
                    pltpu.VMEM((4 * places, width), jnp.bfloat16),
                ],
                flops=2700000000,
                moved=7000000,
            )
        )
    ref_k, ref_v = call(
        ref_kernel,
        (bf16((4 * places, width)), bf16((4 * places, width))),
        (*token_parts, key_weight, value_weight),
        flops=1900000000,
        moved=6000000,
    )
    att, packed_att = call(
        join_kernel,
        (bf16((2, places, width)), bf16((8, 40, width))),
        (*own_parts[0], *own_parts[1], ref_k, ref_v),
        scratch=[pltpu.VMEM((2, 16, width), jnp.float32)],
        flops=500000000,
        moved=4000000,
    )
    att_cells = exchange(packed_att)
    block = call(
        block_kernel,
        bf16((2, places, channels)),
        (lat, att, out_weight, bias),
        flops=500000000,
        moved=3500000,
    )
    codes = position_codes(channels)
    tail_codes = np.repeat(
        np.pad(codes.reshape(8, 2, channels), ((0, 0), (0, 2), (0, 0))), 2, axis=1
    ).reshape(64, channels)
    rows = 320
    heads = call(
        motion_kernel,
        bf16((8, 40, width)),
        (
            lat_cells,
            att_cells,
            out_weight,
            bias,
            motion,
            jnp.asarray(codes),
            jnp.asarray(tail_codes),
            motion_query,
            motion_key,
            motion_value,
        ),
        scratch=[
            pltpu.VMEM((rows, channels), jnp.bfloat16),
            pltpu.VMEM((rows, width), jnp.bfloat16),
            pltpu.VMEM((rows, width), jnp.bfloat16),
            pltpu.VMEM((rows, width), jnp.bfloat16),
        ],
        flops=2500000000,
        moved=9000000,
    )
    returned = exchange(heads)
    motion_heads = call(
        place_kernel,
        bf16((2, places, width)),
        (returned,),
        scratch=[pltpu.VMEM((2, 16, width), jnp.float32)],
        moved=800000,
    )
    return (
        block.reshape(frames, row_count, col_count, channels),
        motion_heads.reshape(frames, row_count, col_count, width),
    )


def solution(mesh):
    return jax.shard_map(
        body,
        mesh=mesh,
        in_specs=(P("tm", "rows", None, None), P(("tm", "rows"), None)) + (P(),) * 10,
        out_specs=(P("tm", "rows", None, None), P("tm", "rows", None, None)),
        check_vma=False,
    )
```

```python
import functools
import math

import jax
import jax.numpy as jnp
import numpy as np
from jax import lax
from jax.experimental import pallas as pl
from jax.experimental.pallas import tpu as pltpu
from jax.sharding import PartitionSpec as P

GROUPS = 32
HEADS = 4
HD = 160
SHOT = 16
WINDOWS = tuple(HD * h // 128 * 128 for h in range(HEADS))
SCALE = math.log2(math.e) / math.sqrt(HD)
AXES = ("tm", "rows")
MAIN = 16
NT = (((1,), (1,)), ((), ()))
VMEM = 20 * 1024 * 1024


def mesh_perm(move):
    def flat(yl, x, z, yh, c):
        return ((yl * 4 + x) * 8 + z) * 4 + yh * 2 + c

    places = [
        (yl, x, z, yh, c)
        for yl in range(2)
        for x in range(4)
        for z in range(8)
        for yh in range(2)
        for c in range(2)
    ]
    return [(flat(*p), flat(*move(*p))) for p in places]


Y_FLIP = mesh_perm(lambda yl, x, z, yh, c: (yl, x, z, 1 - yh, c))
C_FLIP = mesh_perm(lambda yl, x, z, yh, c: (yl, x, z, yh, 1 - c))


def z_perm(step):
    return mesh_perm(
        lambda yl, x, z, yh, c: (yl, x, (z + (step if c == 0 else 8 - step)) % 8, yh, c)
    )


def send(value, pairs):
    return lax.ppermute(value, AXES, pairs)


def shot_groups():
    return [list(range(8 * g, 8 * g + 8)) for g in range(8)]


def exchange(value):
    return lax.all_to_all(value, "tm", 0, 0, axis_index_groups=shot_groups(), tiled=True)


def position_codes(channels):
    halves = np.arange(channels // 2, dtype=np.float64)
    rates = np.exp(-math.log(10000.0) * 2.0 * halves / channels)
    angles = np.arange(SHOT, dtype=np.float64)[:, None] * rates[None, :]
    return np.stack([np.sin(angles), np.cos(angles)], axis=-1).reshape(SHOT, channels).astype(
        np.float32
    )


def call(
    kernel, out_shape, args, in_specs=None, out_specs=None, scratch=(), flops=0, moved=0
):
    return pl.pallas_call(
        kernel,
        out_shape=out_shape,
        grid=(1,),
        in_specs=in_specs or [whole(a) for a in args],
        out_specs=out_specs or jax.tree.map(whole, out_shape),
        scratch_shapes=scratch,
        compiler_params=pltpu.CompilerParams(vmem_limit_bytes=VMEM),
        cost_estimate=pl.CostEstimate(flops=flops, bytes_accessed=moved, transcendentals=0),
    )(*args)


def whole(a):
    rank = len(a.shape)
    return pl.BlockSpec(a.shape, lambda i: (0,) * rank)


def head_window(x, h):
    w = WINDOWS[h]
    part = x[:, w : w + 256]
    lane = lax.broadcasted_iota(jnp.int32, part.shape, 1)
    low = HD * h - w
    return jnp.where((lane >= low) & (lane < low + HD), part, jnp.zeros_like(part))


def side_by_side(parts):
    lane = lax.broadcasted_iota(jnp.int32, (parts[0].shape[0], 128), 1)
    cols = [parts[0][:, :128]]
    for h in range(1, HEADS):
        edge = HD * h - WINDOWS[h]
        cols.append(jnp.where(lane < edge, parts[h - 1][:, 128:], parts[h][:, :128]))
    cols.append(parts[HEADS - 1][:, 128:])
    return jnp.concatenate(cols, axis=1)


def dot(a, b):
    return jnp.dot(a, b, preferred_element_type=jnp.float32)


def split_rows(x):
    high = x.astype(jnp.bfloat16).astype(jnp.float32)
    middle = (x - high).astype(jnp.bfloat16).astype(jnp.float32)
    return jnp.concatenate([high, middle, x - high - middle], axis=0).astype(jnp.bfloat16)


def join_rows(x):
    return x[0:8] + x[8:16] + x[16:24]


def group_stats(sums, count):
    channels = sums.shape[1]
    width = channels // GROUPS
    ch = lax.broadcasted_iota(jnp.int32, (channels, 128), 0)
    gr = lax.broadcasted_iota(jnp.int32, (channels, 128), 1) * width
    member = jnp.where((ch >= gr) & (ch < gr + width), 1.0, 0.0).astype(jnp.bfloat16)
    zeros = jnp.zeros((4, channels), jnp.float32)
    grouped = join_rows(dot(split_rows(jnp.concatenate([sums, zeros], axis=0)), member)) / count
    mean = grouped[0:2]
    rstd = lax.rsqrt(grouped[2:4] - mean * mean + 1e-05)
    both = jnp.concatenate([mean, rstd, jnp.zeros((4, 128), jnp.float32)], axis=0)
    return join_rows(
        lax.dot_general(split_rows(both), member, NT, preferred_element_type=jnp.float32)
    )


def own_kernel(
    lat, peer_c, peer_y, peer_yc, gain, wkv, wq, q_out, o_out, ml_out, xn, kv
):
    _, places, channels = lat.shape
    width = channels // 2
    everyone = (lat, peer_c, peer_y, peer_yc)
    cells = len(everyone) * places
    sums, squares = [], []
    for f in range(2):
        s1 = jnp.zeros((1, channels), jnp.float32)
        s2 = jnp.zeros((1, channels), jnp.float32)
        for piece in everyone:
            x = piece[f].astype(jnp.float32)
            s1 += jnp.sum(x, axis=0, keepdims=True)
            s2 += jnp.sum(x * x, axis=0, keepdims=True)
        sums.append(s1)
        squares.append(s2)
    stats = group_stats(jnp.concatenate(sums + squares, axis=0), cells * (channels // GROUPS))
    for f in range(2):
        mean = stats[f : f + 1]
        scale = stats[2 + f : 3 + f] * gain[...]
        for i, piece in enumerate(everyone):
            at = f * cells + i * places
            x = (piece[f].astype(jnp.float32) - mean) * scale
            xn[at : at + places, :] = x.astype(jnp.bfloat16)
    kv[...] = dot(xn[...], wkv[...]).astype(jnp.bfloat16)
    lane = lax.broadcasted_iota(jnp.int32, (places, 128), 1)
    for f in range(2):
        mine = slice(f * places, (f + 1) * places)
        keys = slice(f * cells, (f + 1) * cells)
        q = dot(xn[f * cells : f * cells + places, :], wq[...]).astype(jnp.bfloat16)
        q_out[mine, :] = q
        ml = jnp.zeros((places, 128), jnp.float32)
        for h in range(HEADS):
            w = WINDOWS[h]
            s = lax.dot_general(
                head_window(q, h), kv[keys, w : w + 256], NT, preferred_element_type=jnp.float32
            )
            top = jnp.max(s, axis=1, keepdims=True)
            p = jnp.exp2((s - top) * SCALE)
            total = jnp.sum(p, axis=1, keepdims=True)
            o_out[h, mine, :] = dot(p.astype(jnp.bfloat16), kv[keys, width + w : width + w + 256])
            ml = jnp.where(lane == h, top, jnp.where(lane == HEADS + h, total, ml))
        ml_out[mine, :] = ml


def tokens_kernel(own, far, near1, near2, near3, flag, out, rows):
    at = 0
    for part in (own, far, near1, near2, near3):
        rows[at : at + part.shape[0], :] = part[...].astype(jnp.float32)
        at += part.shape[0]
    out[...] = rows[...].astype(jnp.bfloat16)


def join_kernel(
    t0, t1, t2, t3, q, o, ml, lat, bias, gain, codes, wkv, wo, att_out, packed, tokens, kv, tail
):
    places, channels = t0.shape
    width = channels // 2
    for i, t in enumerate((t0, t1, t2, t3)):
        tokens[places * i : places * (i + 1), :] = t[...]
    kv[...] = dot(tokens[...], wkv[...]).astype(jnp.bfloat16)
    parts = []
    for h in range(HEADS):
        w = WINDOWS[h]
        s = lax.dot_general(
            head_window(q[...], h), kv[:, w : w + 256], NT, preferred_element_type=jnp.float32
        )
        before = ml[:, h : h + 1]
        top = jnp.maximum(before, jnp.max(s, axis=1, keepdims=True))
        p = jnp.exp2((s - top) * SCALE)
        keep = jnp.exp2((before - top) * SCALE)
        total = ml[:, HEADS + h : HEADS + h + 1] * keep + jnp.sum(p, axis=1, keepdims=True)
        mixed = o[h] * keep + dot(p.astype(jnp.bfloat16), kv[:, width + w : width + w + 256])
        parts.append(mixed * (1.0 / total))
    att_out[...] = side_by_side(parts).astype(jnp.bfloat16)
    for f in range(2):
        mine = slice(f * places, (f + 1) * places)
        block = lat[f].astype(jnp.float32) + dot(att_out[mine, :], wo[...]) + bias[...]
        block = block.astype(jnp.bfloat16).astype(jnp.float32)
        moving = layer_norm(block, gain[...], codes[f : f + 1, :])
        tail[f] = moving[8 * MAIN :, :]
        moving = moving.astype(jnp.bfloat16)
        for s in range(2):
            for d in range(8):
                at = 2 * MAIN * s + MAIN * f
                packed[d, at : at + MAIN, :] = moving[
                    MAIN * d : MAIN * d + MAIN, width * s : width * s + width
                ]
    for d in range(8):
        rows = [
            tail[f, 2 * d : 2 * d + 2, width * s : width * s + width]
            for s in range(2)
            for f in range(2)
        ]
        packed[d, 4 * MAIN :, :] = jnp.concatenate(rows, axis=0).astype(jnp.bfloat16)


def load(pairs, sems):
    copies = [
        pltpu.make_async_copy(source, target, sems.at[i])
        for i, (source, target) in enumerate(pairs)
    ]
    for copy in copies:
        copy.start()
    return copies


def weights_kernel(wk, wv, wq, wo, mq, mk, mv, wkv, wq_out, wo_out, mqkv, flag, sems):
    width = wk.shape[1]
    copies = load(
        (
            (wk, wkv.at[:, :width]),
            (wv, wkv.at[:, width:]),
            (wq, wq_out),
            (wo, wo_out),
            (mq, mqkv.at[:, :width]),
            (mk, mqkv.at[:, width : 2 * width]),
            (mv, mqkv.at[:, 2 * width :]),
        ),
        sems,
    )
    flag[...] = jnp.zeros_like(flag)
    for copy in copies:
        copy.wait()


def block_kernel(lat, att, bias, wo, after, out):
    places = lat.shape[1]
    for f in range(2):
        mine = slice(f * places, (f + 1) * places)
        out[f] = (
            lat[f].astype(jnp.float32) + dot(att[mine, :], wo[...]) + bias[...]
        ).astype(jnp.bfloat16)


def layer_norm(x, gain, codes):
    mean = jnp.mean(x, axis=-1, keepdims=True)
    centered = x - mean
    var = jnp.mean(centered * centered, axis=-1, keepdims=True)
    return centered * lax.rsqrt(var + 1e-05) * gain + codes


def masked_attention(qkv, rows, same):
    width = qkv.shape[1] // 3
    q = qkv[rows, :width]
    parts = []
    for h in range(HEADS):
        w = WINDOWS[h]
        s = lax.dot_general(
            head_window(q, h),
            qkv[rows, width + w : width + w + 256],
            NT,
            preferred_element_type=jnp.float32,
        )
        s = jnp.where(same, s, -jnp.inf)
        top = jnp.max(s, axis=1, keepdims=True)
        p = jnp.exp2((s - top) * SCALE)
        total = jnp.sum(p, axis=1, keepdims=True)
        values = qkv[rows, 2 * width + w : 2 * width + w + 256]
        parts.append(dot(p.astype(jnp.bfloat16), values) * (1.0 / total))
    return side_by_side(parts)


def motion_kernel(moving, weights, out, x, qkv):
    half = moving.shape[2]
    main_rows = 8 * 2 * MAIN
    tail_rows = 64
    x[:main_rows, :half] = moving[:, : 2 * MAIN, :].reshape(main_rows, half)
    x[:main_rows, half:] = moving[:, 2 * MAIN : 4 * MAIN, :].reshape(main_rows, half)
    tail = moving[:, 4 * MAIN :, :].reshape(tail_rows, half)
    x[main_rows:, :half] = tail
    x[main_rows:, half:] = pltpu.roll(tail.astype(jnp.float32), tail_rows - 4, 0).astype(
        jnp.bfloat16
    )
    qkv[...] = dot(x[...], weights[...]).astype(jnp.bfloat16)
    row = lax.broadcasted_iota(jnp.int32, (main_rows, main_rows), 0)
    col = lax.broadcasted_iota(jnp.int32, (main_rows, main_rows), 1)
    heads = masked_attention(
        qkv, slice(0, main_rows), (row & 15) == (col & 15)
    ).astype(jnp.bfloat16)
    out[:, : 2 * MAIN, :] = heads.reshape(8, 2 * MAIN, half)
    row = lax.broadcasted_iota(jnp.int32, (tail_rows, tail_rows), 0)
    col = lax.broadcasted_iota(jnp.int32, (tail_rows, tail_rows), 1)
    heads = masked_attention(
        qkv, slice(main_rows, main_rows + tail_rows), ((row ^ col) & 5) == 0
    ).astype(jnp.bfloat16)
    out[:, 2 * MAIN :, :] = heads.reshape(8, 8, half)


def place_kernel(packed, out, tail):
    for d in range(8):
        for f in range(2):
            out[f, MAIN * d : MAIN * d + MAIN, :] = packed[d, MAIN * f : MAIN * f + MAIN, :]
        rest = packed[d, 2 * MAIN :, :].astype(jnp.float32)
        for f in range(2):
            tail[f, 2 * d : 2 * d + 2, :] = rest[2 * f : 2 * f + 2, :]
    for f in range(2):
        out[f, 8 * MAIN :, :] = tail[f].astype(jnp.bfloat16)


def body(
    latents,
    reference_features,
    norm_gain,
    query_weight,
    key_weight,
    value_weight,
    out_weight,
    out_bias,
    motion_gain,
    motion_query,
    motion_key,
    motion_value,
):
    frames, row_count, col_count, channels = latents.shape
    places = row_count * col_count
    width = query_weight.shape[1]
    bf16 = functools.partial(jax.ShapeDtypeStruct, dtype=jnp.bfloat16)
    f32 = functools.partial(jax.ShapeDtypeStruct, dtype=jnp.float32)
    lat = latents.reshape(frames, places, channels)
    gain = norm_gain.reshape(1, channels)
    bias = out_bias.reshape(1, channels)
    motion = motion_gain.reshape(1, channels)

    hbm = pl.BlockSpec(memory_space=pltpu.HBM)
    vmem = pl.BlockSpec(memory_space=pltpu.VMEM)

    def in_hbm(*arrays):
        return tuple(pltpu.with_memory_space_constraint(a, pltpu.HBM) for a in arrays)

    def in_vmem(*arrays):
        return tuple(pltpu.with_memory_space_constraint(a, pltpu.VMEM) for a in arrays)

    def specs(args, held):
        kept = len(args) - held
        return [whole(a) for a in args[:kept]] + [vmem] * held

    def resident(shape):
        return pltpu.VMEM(shape, jnp.bfloat16)

    from_y = send(lat, Y_FLIP)
    from_c = send(lat, C_FLIP)
    own = reference_features
    chip = jnp.concatenate([own, send(own, C_FLIP)], axis=0)
    frame = 2 * (lax.axis_index("tm") % 8)
    codes = lax.dynamic_slice_in_dim(jnp.asarray(position_codes(channels)), frame, 2)
    own_later, chip, codes = lax.optimization_barrier((own, chip, codes))
    from_z = [send(own_later, z_perm(4))] + [send(chip, z_perm(step)) for step in (1, 2, 3)]

    wkv, wq, wo, motion_qkv, flag = call(
        weights_kernel,
        (
            resident((channels, 2 * width)),
            resident((channels, width)),
            resident((width, channels)),
            resident((channels, 3 * width)),
            bf16((16, 128)),
        ),
        in_hbm(
            key_weight,
            value_weight,
            query_weight,
            out_weight,
            motion_query,
            motion_key,
            motion_value,
        ),
        in_specs=[hbm] * 7,
        out_specs=(vmem,) * 4 + (whole(bf16((16, 128))),),
        scratch=[pltpu.SemaphoreType.DMA((7,))],
        moved=11500000,
    )
    tokens = call(
        tokens_kernel,
        bf16((places, channels)),
        (own, *from_z, flag),
        scratch=[pltpu.VMEM((places, channels), jnp.float32)],
        moved=700000,
    )
    from_y, tokens = lax.optimization_barrier((from_y, tokens))
    from_yc = send(from_y, C_FLIP)
    tokens_y = send(tokens, Y_FLIP)
    tokens_c = send(tokens, C_FLIP)

    args = (lat, from_c, from_y, from_yc, gain) + in_vmem(wkv, wq)
    own_parts = call(
        own_kernel,
        (
            bf16((2 * places, width)),
            f32((HEADS, 2 * places, 256)),
            f32((2 * places, 128)),
        ),
        args,
        in_specs=specs(args, 2),
        scratch=[
            pltpu.VMEM((8 * places, channels), jnp.bfloat16),
            pltpu.VMEM((8 * places, channels), jnp.bfloat16),
        ],
        flops=5400000000,
        moved=9000000,
    )
    tokens_y, own_parts = lax.optimization_barrier((tokens_y, own_parts))
    tokens_yc = send(tokens_y, C_FLIP)
    args = (tokens, tokens_c, tokens_y, tokens_yc, *own_parts, lat, bias, motion, codes)
    args += in_vmem(wkv, wo)
    att, packed = call(
        join_kernel,
        (bf16((2 * places, width)), pltpu.HBM((8, 72, width), jnp.bfloat16)),
        args,
        in_specs=specs(args, 2),
        scratch=[
            pltpu.VMEM((4 * places, channels), jnp.bfloat16),
            pltpu.VMEM((4 * places, channels), jnp.bfloat16),
            pltpu.VMEM((2, 16, channels), jnp.float32),
        ],
        flops=2900000000,
        moved=8000000,
    )
    moving = exchange(packed)
    args = (moving,) + in_vmem(motion_qkv)
    rows = 320
    heads = call(
        motion_kernel,
        pltpu.HBM((8, 40, width), jnp.bfloat16),
        args,
        in_specs=specs(args, 1),
        scratch=[
            pltpu.VMEM((rows, channels), jnp.bfloat16),
            pltpu.VMEM((rows, 3 * width), jnp.bfloat16),
        ],
        flops=2200000000,
        moved=8000000,
    )
    returned = exchange(heads)
    args = (lat, att, bias, out_weight, heads)
    block = call(
        block_kernel,
        bf16((2, places, channels)),
        args,
        in_specs=[whole(a) for a in args[:4]] + [hbm],
        flops=500000000,
        moved=3000000,
    )
    motion_heads = call(
        place_kernel,
        bf16((2, places, width)),
        (returned,),
        scratch=[pltpu.VMEM((2, 16, width), jnp.float32)],
        moved=800000,
    )
    return (
        block.reshape(frames, row_count, col_count, channels),
        motion_heads.reshape(frames, row_count, col_count, width),
    )


def solution(mesh):
    return jax.shard_map(
        body,
        mesh=mesh,
        in_specs=(P("tm", "rows", None, None), P(("tm", "rows"), None)) + (P(),) * 10,
        out_specs=(P("tm", "rows", None, None), P("tm", "rows", None, None)),
        check_vma=False,
    )
```

```python
import functools
import math

import jax
import jax.numpy as jnp
import numpy as np
from jax import lax
from jax.experimental import pallas as pl
from jax.experimental.pallas import tpu as pltpu
from jax.sharding import PartitionSpec as P

GROUPS = 32
HEADS = 4
HD = 160
SHOT = 16
WINDOWS = tuple(HD * h // 128 * 128 for h in range(HEADS))
SCALE = math.log2(math.e) / math.sqrt(HD)
AXES = ("tm", "rows")
MAIN = 16
NT = (((1,), (1,)), ((), ()))
VMEM = 20 * 1024 * 1024


def mesh_perm(move):
    def flat(yl, x, z, yh, c):
        return ((yl * 4 + x) * 8 + z) * 4 + yh * 2 + c

    places = [
        (yl, x, z, yh, c)
        for yl in range(2)
        for x in range(4)
        for z in range(8)
        for yh in range(2)
        for c in range(2)
    ]
    return [(flat(*p), flat(*move(*p))) for p in places]


Y_FLIP = mesh_perm(lambda yl, x, z, yh, c: (yl, x, z, 1 - yh, c))
C_FLIP = mesh_perm(lambda yl, x, z, yh, c: (yl, x, z, yh, 1 - c))


def z_perm(step):
    return mesh_perm(
        lambda yl, x, z, yh, c: (yl, x, (z + (step if c == 0 else 8 - step)) % 8, yh, c)
    )


def send(value, pairs):
    return lax.ppermute(value, AXES, pairs)


def shot_groups():
    return [list(range(8 * g, 8 * g + 8)) for g in range(8)]


def exchange(value):
    return lax.all_to_all(value, "tm", 0, 0, axis_index_groups=shot_groups(), tiled=True)


def position_codes(channels):
    halves = np.arange(channels // 2, dtype=np.float64)
    rates = np.exp(-math.log(10000.0) * 2.0 * halves / channels)
    angles = np.arange(SHOT, dtype=np.float64)[:, None] * rates[None, :]
    return np.stack([np.sin(angles), np.cos(angles)], axis=-1).reshape(SHOT, channels).astype(
        np.float32
    )


def call(
    kernel, out_shape, args, in_specs=None, out_specs=None, scratch=(), flops=0, moved=0
):
    return pl.pallas_call(
        kernel,
        out_shape=out_shape,
        grid=(1,),
        in_specs=in_specs or [whole(a) for a in args],
        out_specs=out_specs or jax.tree.map(whole, out_shape),
        scratch_shapes=scratch,
        compiler_params=pltpu.CompilerParams(vmem_limit_bytes=VMEM),
        cost_estimate=pl.CostEstimate(flops=flops, bytes_accessed=moved, transcendentals=0),
    )(*args)


def whole(a):
    rank = len(a.shape)
    return pl.BlockSpec(a.shape, lambda i: (0,) * rank)


def head_window(x, h):
    w = WINDOWS[h]
    part = x[:, w : w + 256]
    lane = lax.broadcasted_iota(jnp.int32, part.shape, 1)
    low = HD * h - w
    return jnp.where((lane >= low) & (lane < low + HD), part, jnp.zeros_like(part))


def side_by_side(parts):
    lane = lax.broadcasted_iota(jnp.int32, (parts[0].shape[0], 128), 1)
    cols = [parts[0][:, :128]]
    for h in range(1, HEADS):
        edge = HD * h - WINDOWS[h]
        cols.append(jnp.where(lane < edge, parts[h - 1][:, 128:], parts[h][:, :128]))
    cols.append(parts[HEADS - 1][:, 128:])
    return jnp.concatenate(cols, axis=1)


def dot(a, b):
    return jnp.dot(a, b, preferred_element_type=jnp.float32)


def split_rows(x):
    high = x.astype(jnp.bfloat16).astype(jnp.float32)
    middle = (x - high).astype(jnp.bfloat16).astype(jnp.float32)
    return jnp.concatenate([high, middle, x - high - middle], axis=0).astype(jnp.bfloat16)


def join_rows(x):
    return x[0:8] + x[8:16] + x[16:24]


def group_stats(sums, count):
    channels = sums.shape[1]
    width = channels // GROUPS
    ch = lax.broadcasted_iota(jnp.int32, (channels, 128), 0)
    gr = lax.broadcasted_iota(jnp.int32, (channels, 128), 1) * width
    member = jnp.where((ch >= gr) & (ch < gr + width), 1.0, 0.0).astype(jnp.bfloat16)
    zeros = jnp.zeros((4, channels), jnp.float32)
    grouped = join_rows(dot(split_rows(jnp.concatenate([sums, zeros], axis=0)), member)) / count
    mean = grouped[0:2]
    rstd = lax.rsqrt(grouped[2:4] - mean * mean + 1e-05)
    both = jnp.concatenate([mean, rstd, jnp.zeros((4, 128), jnp.float32)], axis=0)
    return join_rows(
        lax.dot_general(split_rows(both), member, NT, preferred_element_type=jnp.float32)
    )


def own_kernel(
    lat, peer_c, peer_y, peer_yc, gain, wkv, wq, q_out, o_out, ml_out, xn, kv
):
    _, places, channels = lat.shape
    width = channels // 2
    everyone = (lat, peer_c, peer_y, peer_yc)
    cells = len(everyone) * places
    sums, squares = [], []
    for f in range(2):
        s1 = jnp.zeros((1, channels), jnp.float32)
        s2 = jnp.zeros((1, channels), jnp.float32)
        for piece in everyone:
            x = piece[f].astype(jnp.float32)
            s1 += jnp.sum(x, axis=0, keepdims=True)
            s2 += jnp.sum(x * x, axis=0, keepdims=True)
        sums.append(s1)
        squares.append(s2)
    stats = group_stats(jnp.concatenate(sums + squares, axis=0), cells * (channels // GROUPS))
    for f in range(2):
        mean = stats[f : f + 1]
        scale = stats[2 + f : 3 + f] * gain[...]
        for i, piece in enumerate(everyone):
            at = f * cells + i * places
            x = (piece[f].astype(jnp.float32) - mean) * scale
            xn[at : at + places, :] = x.astype(jnp.bfloat16)
    kv[...] = dot(xn[...], wkv[...]).astype(jnp.bfloat16)
    lane = lax.broadcasted_iota(jnp.int32, (places, 128), 1)
    for f in range(2):
        mine = slice(f * places, (f + 1) * places)
        keys = slice(f * cells, (f + 1) * cells)
        q = dot(xn[f * cells : f * cells + places, :], wq[...]).astype(jnp.bfloat16)
        q_out[mine, :] = q
        ml = jnp.zeros((places, 128), jnp.float32)
        for h in range(HEADS):
            w = WINDOWS[h]
            s = lax.dot_general(
                head_window(q, h), kv[keys, w : w + 256], NT, preferred_element_type=jnp.float32
            )
            top = jnp.max(s, axis=1, keepdims=True)
            p = jnp.exp2((s - top) * SCALE)
            total = jnp.sum(p, axis=1, keepdims=True)
            o_out[h, mine, :] = dot(p.astype(jnp.bfloat16), kv[keys, width + w : width + w + 256])
            ml = jnp.where(lane == h, top, jnp.where(lane == HEADS + h, total, ml))
        ml_out[mine, :] = ml


def tokens_kernel(own, far, near1, near2, near3, flag, out, rows):
    at = 0
    for part in (own, far, near1, near2, near3):
        rows[at : at + part.shape[0], :] = part[...].astype(jnp.float32)
        at += part.shape[0]
    out[...] = rows[...].astype(jnp.bfloat16)


def join_kernel(
    t0, t1, t2, t3, q, o, ml, lat, bias, gain, codes, wkv, wo, block_out, packed, tokens, kv, tail
):
    places, channels = t0.shape
    width = channels // 2
    for i, t in enumerate((t0, t1, t2, t3)):
        tokens[places * i : places * (i + 1), :] = t[...]
    kv[...] = dot(tokens[...], wkv[...]).astype(jnp.bfloat16)
    parts = []
    for h in range(HEADS):
        w = WINDOWS[h]
        s = lax.dot_general(
            head_window(q[...], h), kv[:, w : w + 256], NT, preferred_element_type=jnp.float32
        )
        before = ml[:, h : h + 1]
        top = jnp.maximum(before, jnp.max(s, axis=1, keepdims=True))
        p = jnp.exp2((s - top) * SCALE)
        keep = jnp.exp2((before - top) * SCALE)
        total = ml[:, HEADS + h : HEADS + h + 1] * keep + jnp.sum(p, axis=1, keepdims=True)
        mixed = o[h] * keep + dot(p.astype(jnp.bfloat16), kv[:, width + w : width + w + 256])
        parts.append(mixed * (1.0 / total))
    att = side_by_side(parts).astype(jnp.bfloat16)
    for f in range(2):
        mine = slice(f * places, (f + 1) * places)
        block = lat[f].astype(jnp.float32) + dot(att[mine, :], wo[...]) + bias[...]
        block = block.astype(jnp.bfloat16)
        block_out[f] = block
        block = block.astype(jnp.float32)
        moving = layer_norm(block, gain[...], codes[f : f + 1, :])
        tail[f] = moving[8 * MAIN :, :]
        moving = moving.astype(jnp.bfloat16)
        for s in range(2):
            for d in range(8):
                at = 2 * MAIN * s + MAIN * f
                packed[d, at : at + MAIN, :] = moving[
                    MAIN * d : MAIN * d + MAIN, width * s : width * s + width
                ]
    for d in range(8):
        rows = [
            tail[f, 2 * d : 2 * d + 2, width * s : width * s + width]
            for s in range(2)
            for f in range(2)
        ]
        packed[d, 4 * MAIN :, :] = jnp.concatenate(rows, axis=0).astype(jnp.bfloat16)


def load(pairs, sems):
    copies = [
        pltpu.make_async_copy(source, target, sems.at[i])
        for i, (source, target) in enumerate(pairs)
    ]
    for copy in copies:
        copy.start()
    return copies


def weights_kernel(wk, wv, wq, wo, mq, mk, mv, wkv, wq_out, wo_out, mqkv, flag, sems):
    width = wk.shape[1]
    copies = load(
        (
            (wk, wkv.at[:, :width]),
            (wv, wkv.at[:, width:]),
            (wq, wq_out),
            (wo, wo_out),
            (mq, mqkv.at[:, :width]),
            (mk, mqkv.at[:, width : 2 * width]),
            (mv, mqkv.at[:, 2 * width :]),
        ),
        sems,
    )
    flag[...] = jnp.zeros_like(flag)
    for copy in copies:
        copy.wait()


def layer_norm(x, gain, codes):
    mean = jnp.mean(x, axis=-1, keepdims=True)
    centered = x - mean
    var = jnp.mean(centered * centered, axis=-1, keepdims=True)
    return centered * lax.rsqrt(var + 1e-05) * gain + codes


def masked_attention(qkv, rows, same):
    width = qkv.shape[1] // 3
    q = qkv[rows, :width]
    parts = []
    for h in range(HEADS):
        w = WINDOWS[h]
        s = lax.dot_general(
            head_window(q, h),
            qkv[rows, width + w : width + w + 256],
            NT,
            preferred_element_type=jnp.float32,
        )
        s = jnp.where(same, s, -jnp.inf)
        top = jnp.max(s, axis=1, keepdims=True)
        p = jnp.exp2((s - top) * SCALE)
        total = jnp.sum(p, axis=1, keepdims=True)
        values = qkv[rows, 2 * width + w : 2 * width + w + 256]
        parts.append(dot(p.astype(jnp.bfloat16), values) * (1.0 / total))
    return side_by_side(parts)


def motion_kernel(moving, weights, out, x, qkv):
    half = moving.shape[2]
    main_rows = 8 * 2 * MAIN
    tail_rows = 64
    x[:main_rows, :half] = moving[:, : 2 * MAIN, :].reshape(main_rows, half)
    x[:main_rows, half:] = moving[:, 2 * MAIN : 4 * MAIN, :].reshape(main_rows, half)
    tail = moving[:, 4 * MAIN :, :].reshape(tail_rows, half)
    x[main_rows:, :half] = tail
    x[main_rows:, half:] = pltpu.roll(tail.astype(jnp.float32), tail_rows - 4, 0).astype(
        jnp.bfloat16
    )
    qkv[...] = dot(x[...], weights[...]).astype(jnp.bfloat16)
    row = lax.broadcasted_iota(jnp.int32, (main_rows, main_rows), 0)
    col = lax.broadcasted_iota(jnp.int32, (main_rows, main_rows), 1)
    heads = masked_attention(
        qkv, slice(0, main_rows), (row & 15) == (col & 15)
    ).astype(jnp.bfloat16)
    out[:, : 2 * MAIN, :] = heads.reshape(8, 2 * MAIN, half)
    row = lax.broadcasted_iota(jnp.int32, (tail_rows, tail_rows), 0)
    col = lax.broadcasted_iota(jnp.int32, (tail_rows, tail_rows), 1)
    heads = masked_attention(
        qkv, slice(main_rows, main_rows + tail_rows), ((row ^ col) & 5) == 0
    ).astype(jnp.bfloat16)
    out[:, 2 * MAIN :, :] = heads.reshape(8, 8, half)


def place_kernel(packed, out, tail):
    for d in range(8):
        for f in range(2):
            out[f, MAIN * d : MAIN * d + MAIN, :] = packed[d, MAIN * f : MAIN * f + MAIN, :]
        rest = packed[d, 2 * MAIN :, :].astype(jnp.float32)
        for f in range(2):
            tail[f, 2 * d : 2 * d + 2, :] = rest[2 * f : 2 * f + 2, :]
    for f in range(2):
        out[f, 8 * MAIN :, :] = tail[f].astype(jnp.bfloat16)


def body(
    latents,
    reference_features,
    norm_gain,
    query_weight,
    key_weight,
    value_weight,
    out_weight,
    out_bias,
    motion_gain,
    motion_query,
    motion_key,
    motion_value,
):
    frames, row_count, col_count, channels = latents.shape
    places = row_count * col_count
    width = query_weight.shape[1]
    bf16 = functools.partial(jax.ShapeDtypeStruct, dtype=jnp.bfloat16)
    f32 = functools.partial(jax.ShapeDtypeStruct, dtype=jnp.float32)
    lat = latents.reshape(frames, places, channels)
    gain = norm_gain.reshape(1, channels)
    bias = out_bias.reshape(1, channels)
    motion = motion_gain.reshape(1, channels)

    hbm = pl.BlockSpec(memory_space=pltpu.HBM)
    vmem = pl.BlockSpec(memory_space=pltpu.VMEM)

    def in_hbm(*arrays):
        return tuple(pltpu.with_memory_space_constraint(a, pltpu.HBM) for a in arrays)

    def in_vmem(*arrays):
        return tuple(pltpu.with_memory_space_constraint(a, pltpu.VMEM) for a in arrays)

    def specs(args, held):
        kept = len(args) - held
        return [whole(a) for a in args[:kept]] + [vmem] * held

    def resident(shape):
        return pltpu.VMEM(shape, jnp.bfloat16)

    from_y = send(lat, Y_FLIP)
    from_c = send(lat, C_FLIP)
    own = reference_features
    chip = jnp.concatenate([own, send(own, C_FLIP)], axis=0)
    frame = 2 * (lax.axis_index("tm") % 8)
    codes = lax.dynamic_slice_in_dim(jnp.asarray(position_codes(channels)), frame, 2)
    own_later, chip, codes = lax.optimization_barrier((own, chip, codes))
    from_z = [send(own_later, z_perm(4))] + [send(chip, z_perm(step)) for step in (1, 2, 3)]

    wkv, wq, wo, motion_qkv, flag = call(
        weights_kernel,
        (
            resident((channels, 2 * width)),
            resident((channels, width)),
            resident((width, channels)),
            resident((channels, 3 * width)),
            bf16((16, 128)),
        ),
        in_hbm(
            key_weight,
            value_weight,
            query_weight,
            out_weight,
            motion_query,
            motion_key,
            motion_value,
        ),
        in_specs=[hbm] * 7,
        out_specs=(vmem,) * 4 + (whole(bf16((16, 128))),),
        scratch=[pltpu.SemaphoreType.DMA((7,))],
        moved=11500000,
    )
    tokens = call(
        tokens_kernel,
        bf16((places, channels)),
        (own, *from_z, flag),
        scratch=[pltpu.VMEM((places, channels), jnp.float32)],
        moved=700000,
    )
    from_y, tokens = lax.optimization_barrier((from_y, tokens))
    from_yc = send(from_y, C_FLIP)
    tokens_y = send(tokens, Y_FLIP)
    tokens_c = send(tokens, C_FLIP)

    args = (lat, from_c, from_y, from_yc, gain) + in_vmem(wkv, wq)
    own_parts = call(
        own_kernel,
        (
            bf16((2 * places, width)),
            f32((HEADS, 2 * places, 256)),
            f32((2 * places, 128)),
        ),
        args,
        in_specs=specs(args, 2),
        scratch=[
            pltpu.VMEM((8 * places, channels), jnp.bfloat16),
            pltpu.VMEM((8 * places, channels), jnp.bfloat16),
        ],
        flops=5400000000,
        moved=9000000,
    )
    tokens_y, own_parts = lax.optimization_barrier((tokens_y, own_parts))
    tokens_yc = send(tokens_y, C_FLIP)
    args = (tokens, tokens_c, tokens_y, tokens_yc, *own_parts, lat, bias, motion, codes)
    args += in_vmem(wkv, wo)
    block, packed = call(
        join_kernel,
        (bf16((2, places, channels)), bf16((8, 72, width))),
        args,
        in_specs=specs(args, 2),
        scratch=[
            pltpu.VMEM((4 * places, channels), jnp.bfloat16),
            pltpu.VMEM((4 * places, channels), jnp.bfloat16),
            pltpu.VMEM((2, 16, channels), jnp.float32),
        ],
        flops=2900000000,
        moved=8000000,
    )
    moving = exchange(packed)
    args = (moving,) + in_vmem(motion_qkv)
    rows = 320
    heads = call(
        motion_kernel,
        bf16((8, 40, width)),
        args,
        in_specs=specs(args, 1),
        scratch=[
            pltpu.VMEM((rows, channels), jnp.bfloat16),
            pltpu.VMEM((rows, 3 * width), jnp.bfloat16),
        ],
        flops=2200000000,
        moved=8000000,
    )
    returned = exchange(heads)
    motion_heads = call(
        place_kernel,
        bf16((2, places, width)),
        (returned,),
        scratch=[pltpu.VMEM((2, 16, width), jnp.float32)],
        moved=800000,
    )
    return (
        block.reshape(frames, row_count, col_count, channels),
        motion_heads.reshape(frames, row_count, col_count, width),
    )


def solution(mesh):
    return jax.shard_map(
        body,
        mesh=mesh,
        in_specs=(P("tm", "rows", None, None), P(("tm", "rows"), None)) + (P(),) * 10,
        out_specs=(P("tm", "rows", None, None), P("tm", "rows", None, None)),
        check_vma=False,
    )
```

```python
import functools
import math

import jax
import jax.numpy as jnp
import numpy as np
from jax import lax
from jax.experimental import pallas as pl
from jax.experimental.pallas import tpu as pltpu
from jax.sharding import PartitionSpec as P

GROUPS = 32
HEADS = 4
HD = 160
SHOT = 16
WINDOWS = tuple(HD * h // 128 * 128 for h in range(HEADS))
SCALE = math.log2(math.e) / math.sqrt(HD)
AXES = ("tm", "rows")
MAIN = 16
NT = (((1,), (1,)), ((), ()))
VMEM = 20 * 1024 * 1024


def mesh_perm(move):
    def flat(yl, x, z, yh, c):
        return ((yl * 4 + x) * 8 + z) * 4 + yh * 2 + c

    places = [
        (yl, x, z, yh, c)
        for yl in range(2)
        for x in range(4)
        for z in range(8)
        for yh in range(2)
        for c in range(2)
    ]
    return [(flat(*p), flat(*move(*p))) for p in places]


Y_FLIP = mesh_perm(lambda yl, x, z, yh, c: (yl, x, z, 1 - yh, c))
C_FLIP = mesh_perm(lambda yl, x, z, yh, c: (yl, x, z, yh, 1 - c))


def z_perm(step):
    return mesh_perm(
        lambda yl, x, z, yh, c: (yl, x, (z + (step if c == 0 else 8 - step)) % 8, yh, c)
    )


def send(value, pairs):
    return lax.ppermute(value, AXES, pairs)


def shot_groups():
    return [list(range(8 * g, 8 * g + 8)) for g in range(8)]


def exchange(value):
    return lax.all_to_all(value, "tm", 0, 0, axis_index_groups=shot_groups(), tiled=True)


def position_codes(channels):
    halves = np.arange(channels // 2, dtype=np.float64)
    rates = np.exp(-math.log(10000.0) * 2.0 * halves / channels)
    angles = np.arange(SHOT, dtype=np.float64)[:, None] * rates[None, :]
    return np.stack([np.sin(angles), np.cos(angles)], axis=-1).reshape(SHOT, channels).astype(
        np.float32
    )


def call(
    kernel, out_shape, args, in_specs=None, out_specs=None, scratch=(), flops=0, moved=0
):
    return pl.pallas_call(
        kernel,
        out_shape=out_shape,
        grid=(1,),
        in_specs=in_specs or [whole(a) for a in args],
        out_specs=out_specs or jax.tree.map(whole, out_shape),
        scratch_shapes=scratch,
        compiler_params=pltpu.CompilerParams(vmem_limit_bytes=VMEM),
        cost_estimate=pl.CostEstimate(flops=flops, bytes_accessed=moved, transcendentals=0),
    )(*args)


def whole(a):
    rank = len(a.shape)
    return pl.BlockSpec(a.shape, lambda i: (0,) * rank)


def head_window(x, h):
    w = WINDOWS[h]
    part = x[:, w : w + 256]
    lane = lax.broadcasted_iota(jnp.int32, part.shape, 1)
    low = HD * h - w
    return jnp.where((lane >= low) & (lane < low + HD), part, jnp.zeros_like(part))


def side_by_side(parts):
    lane = lax.broadcasted_iota(jnp.int32, (parts[0].shape[0], 128), 1)
    cols = [parts[0][:, :128]]
    for h in range(1, HEADS):
        edge = HD * h - WINDOWS[h]
        cols.append(jnp.where(lane < edge, parts[h - 1][:, 128:], parts[h][:, :128]))
    cols.append(parts[HEADS - 1][:, 128:])
    return jnp.concatenate(cols, axis=1)


def dot(a, b):
    return jnp.dot(a, b, preferred_element_type=jnp.float32)


def split_rows(x):
    high = x.astype(jnp.bfloat16).astype(jnp.float32)
    middle = (x - high).astype(jnp.bfloat16).astype(jnp.float32)
    return jnp.concatenate([high, middle, x - high - middle], axis=0).astype(jnp.bfloat16)


def join_rows(x):
    return x[0:8] + x[8:16] + x[16:24]


def group_stats(sums, count):
    channels = sums.shape[1]
    width = channels // GROUPS
    ch = lax.broadcasted_iota(jnp.int32, (channels, 128), 0)
    gr = lax.broadcasted_iota(jnp.int32, (channels, 128), 1) * width
    member = jnp.where((ch >= gr) & (ch < gr + width), 1.0, 0.0).astype(jnp.bfloat16)
    zeros = jnp.zeros((4, channels), jnp.float32)
    grouped = join_rows(dot(split_rows(jnp.concatenate([sums, zeros], axis=0)), member)) / count
    mean = grouped[0:2]
    rstd = lax.rsqrt(jnp.maximum(grouped[2:4] - mean * mean, 0.0) + 1e-05)
    both = jnp.concatenate([mean, rstd, jnp.zeros((4, 128), jnp.float32)], axis=0)
    return join_rows(
        lax.dot_general(split_rows(both), member, NT, preferred_element_type=jnp.float32)
    )


def own_kernel(
    lat, peer_c, peer_y, peer_yc, gain, wkv, wq, q_out, o_out, ml_out, xn, kv
):
    _, places, channels = lat.shape
    width = channels // 2
    everyone = (lat, peer_c, peer_y, peer_yc)
    cells = len(everyone) * places
    sums, squares = [], []
    for f in range(2):
        s1 = jnp.zeros((1, channels), jnp.float32)
        s2 = jnp.zeros((1, channels), jnp.float32)
        for piece in everyone:
            x = piece[f].astype(jnp.float32)
            s1 += jnp.sum(x, axis=0, keepdims=True)
            s2 += jnp.sum(x * x, axis=0, keepdims=True)
        sums.append(s1)
        squares.append(s2)
    stats = group_stats(jnp.concatenate(sums + squares, axis=0), cells * (channels // GROUPS))
    for f in range(2):
        mean = stats[f : f + 1]
        scale = stats[2 + f : 3 + f] * gain[...]
        for i, piece in enumerate(everyone):
            at = f * cells + i * places
            x = (piece[f].astype(jnp.float32) - mean) * scale
            xn[at : at + places, :] = x.astype(jnp.bfloat16)
    kv[...] = dot(xn[...], wkv[...]).astype(jnp.bfloat16)
    lane = lax.broadcasted_iota(jnp.int32, (places, 128), 1)
    for f in range(2):
        mine = slice(f * places, (f + 1) * places)
        keys = slice(f * cells, (f + 1) * cells)
        q = dot(xn[f * cells : f * cells + places, :], wq[...]).astype(jnp.bfloat16)
        q_out[mine, :] = q
        ml = jnp.zeros((places, 128), jnp.float32)
        for h in range(HEADS):
            w = WINDOWS[h]
            s = lax.dot_general(
                head_window(q, h), kv[keys, w : w + 256], NT, preferred_element_type=jnp.float32
            )
            top = jnp.max(s, axis=1, keepdims=True)
            p = jnp.exp2((s - top) * SCALE)
            total = jnp.sum(p, axis=1, keepdims=True)
            o_out[h, mine, :] = dot(p.astype(jnp.bfloat16), kv[keys, width + w : width + w + 256])
            ml = jnp.where(lane == h, top, jnp.where(lane == HEADS + h, total, ml))
        ml_out[mine, :] = ml


def tokens_kernel(own, far, near1, near2, near3, flag, out, rows):
    at = 0
    for part in (own, far, near1, near2, near3):
        rows[at : at + part.shape[0], :] = part[...].astype(jnp.float32)
        at += part.shape[0]
    out[...] = rows[...].astype(jnp.bfloat16)


def join_kernel(
    t0, t1, t2, t3, q, o, ml, lat, bias, gain, codes, wkv, wo, block_out, packed, tokens, kv, tail
):
    places, channels = t0.shape
    width = channels // 2
    for i, t in enumerate((t0, t1, t2, t3)):
        tokens[places * i : places * (i + 1), :] = t[...]
    kv[...] = dot(tokens[...], wkv[...]).astype(jnp.bfloat16)
    parts = []
    for h in range(HEADS):
        w = WINDOWS[h]
        s = lax.dot_general(
            head_window(q[...], h), kv[:, w : w + 256], NT, preferred_element_type=jnp.float32
        )
        before = ml[:, h : h + 1]
        top = jnp.maximum(before, jnp.max(s, axis=1, keepdims=True))
        p = jnp.exp2((s - top) * SCALE)
        keep = jnp.exp2((before - top) * SCALE)
        total = ml[:, HEADS + h : HEADS + h + 1] * keep + jnp.sum(p, axis=1, keepdims=True)
        mixed = o[h] * keep + dot(p.astype(jnp.bfloat16), kv[:, width + w : width + w + 256])
        parts.append(mixed * (1.0 / total))
    att = side_by_side(parts).astype(jnp.bfloat16)
    for f in range(2):
        mine = slice(f * places, (f + 1) * places)
        block = lat[f].astype(jnp.float32) + dot(att[mine, :], wo[...]) + bias[...]
        block = block.astype(jnp.bfloat16)
        block_out[f] = block
        block = block.astype(jnp.float32)
        moving = layer_norm(block, gain[...], codes[f : f + 1, :])
        tail[f] = moving[8 * MAIN :, :]
        moving = moving.astype(jnp.bfloat16)
        for s in range(2):
            for d in range(8):
                at = 2 * MAIN * s + MAIN * f
                packed[d, at : at + MAIN, :] = moving[
                    MAIN * d : MAIN * d + MAIN, width * s : width * s + width
                ]
    for d in range(8):
        rows = [
            tail[f, 2 * d : 2 * d + 2, width * s : width * s + width]
            for s in range(2)
            for f in range(2)
        ]
        packed[d, 4 * MAIN :, :] = jnp.concatenate(rows, axis=0).astype(jnp.bfloat16)


def load(pairs, sems):
    copies = [
        pltpu.make_async_copy(source, target, sems.at[i])
        for i, (source, target) in enumerate(pairs)
    ]
    for copy in copies:
        copy.start()
    return copies


def weights_kernel(wk, wv, wq, wo, mq, mk, mv, wkv, wq_out, wo_out, mqkv, flag, sems):
    width = wk.shape[1]
    copies = load(
        (
            (wk, wkv.at[:, :width]),
            (wv, wkv.at[:, width:]),
            (wq, wq_out),
            (wo, wo_out),
            (mq, mqkv.at[:, :width]),
            (mk, mqkv.at[:, width : 2 * width]),
            (mv, mqkv.at[:, 2 * width :]),
        ),
        sems,
    )
    flag[...] = jnp.zeros_like(flag)
    for copy in copies:
        copy.wait()


def layer_norm(x, gain, codes):
    mean = jnp.mean(x, axis=-1, keepdims=True)
    centered = x - mean
    var = jnp.mean(centered * centered, axis=-1, keepdims=True)
    return centered * lax.rsqrt(var + 1e-05) * gain + codes


def masked_attention(qkv, rows, same):
    width = qkv.shape[1] // 3
    q = qkv[rows, :width]
    parts = []
    for h in range(HEADS):
        w = WINDOWS[h]
        s = lax.dot_general(
            head_window(q, h),
            qkv[rows, width + w : width + w + 256],
            NT,
            preferred_element_type=jnp.float32,
        )
        s = jnp.where(same, s, -jnp.inf)
        top = jnp.max(s, axis=1, keepdims=True)
        p = jnp.exp2((s - top) * SCALE)
        total = jnp.sum(p, axis=1, keepdims=True)
        values = qkv[rows, 2 * width + w : 2 * width + w + 256]
        parts.append(dot(p.astype(jnp.bfloat16), values) * (1.0 / total))
    return side_by_side(parts)


def motion_kernel(moving, weights, out, x, qkv):
    half = moving.shape[2]
    main_rows = 8 * 2 * MAIN
    tail_rows = 64
    x[:main_rows, :half] = moving[:, : 2 * MAIN, :].reshape(main_rows, half)
    x[:main_rows, half:] = moving[:, 2 * MAIN : 4 * MAIN, :].reshape(main_rows, half)
    tail = moving[:, 4 * MAIN :, :].reshape(tail_rows, half)
    x[main_rows:, :half] = tail
    x[main_rows:, half:] = pltpu.roll(tail.astype(jnp.float32), tail_rows - 4, 0).astype(
        jnp.bfloat16
    )
    qkv[...] = dot(x[...], weights[...]).astype(jnp.bfloat16)
    row = lax.broadcasted_iota(jnp.int32, (main_rows, main_rows), 0)
    col = lax.broadcasted_iota(jnp.int32, (main_rows, main_rows), 1)
    heads = masked_attention(
        qkv, slice(0, main_rows), (row & 15) == (col & 15)
    ).astype(jnp.bfloat16)
    out[:, : 2 * MAIN, :] = heads.reshape(8, 2 * MAIN, half)
    row = lax.broadcasted_iota(jnp.int32, (tail_rows, tail_rows), 0)
    col = lax.broadcasted_iota(jnp.int32, (tail_rows, tail_rows), 1)
    heads = masked_attention(
        qkv, slice(main_rows, main_rows + tail_rows), ((row ^ col) & 5) == 0
    ).astype(jnp.bfloat16)
    out[:, 2 * MAIN :, :] = heads.reshape(8, 8, half)


def place_kernel(packed, out, tail):
    for d in range(8):
        for f in range(2):
            out[f, MAIN * d : MAIN * d + MAIN, :] = packed[d, MAIN * f : MAIN * f + MAIN, :]
        rest = packed[d, 2 * MAIN :, :].astype(jnp.float32)
        for f in range(2):
            tail[f, 2 * d : 2 * d + 2, :] = rest[2 * f : 2 * f + 2, :]
    for f in range(2):
        out[f, 8 * MAIN :, :] = tail[f].astype(jnp.bfloat16)


def body(
    latents,
    reference_features,
    norm_gain,
    query_weight,
    key_weight,
    value_weight,
    out_weight,
    out_bias,
    motion_gain,
    motion_query,
    motion_key,
    motion_value,
):
    frames, row_count, col_count, channels = latents.shape
    places = row_count * col_count
    width = query_weight.shape[1]
    bf16 = functools.partial(jax.ShapeDtypeStruct, dtype=jnp.bfloat16)
    f32 = functools.partial(jax.ShapeDtypeStruct, dtype=jnp.float32)
    lat = latents.reshape(frames, places, channels)
    gain = norm_gain.reshape(1, channels)
    bias = out_bias.reshape(1, channels)
    motion = motion_gain.reshape(1, channels)

    hbm = pl.BlockSpec(memory_space=pltpu.HBM)
    vmem = pl.BlockSpec(memory_space=pltpu.VMEM)

    def in_hbm(*arrays):
        return tuple(pltpu.with_memory_space_constraint(a, pltpu.HBM) for a in arrays)

    def in_vmem(*arrays):
        return tuple(pltpu.with_memory_space_constraint(a, pltpu.VMEM) for a in arrays)

    def specs(args, held):
        kept = len(args) - held
        return [whole(a) for a in args[:kept]] + [vmem] * held

    def resident(shape):
        return pltpu.VMEM(shape, jnp.bfloat16)

    from_y = send(lat, Y_FLIP)
    from_c = send(lat, C_FLIP)
    own = reference_features
    chip = jnp.concatenate([own, send(own, C_FLIP)], axis=0)
    frame = 2 * (lax.axis_index("tm") % 8)
    codes = lax.dynamic_slice_in_dim(jnp.asarray(position_codes(channels)), frame, 2)
    own_later, chip, codes = lax.optimization_barrier((own, chip, codes))
    from_z = [send(own_later, z_perm(4))] + [send(chip, z_perm(step)) for step in (1, 2, 3)]

    wkv, wq, wo, motion_qkv, flag = call(
        weights_kernel,
        (
            resident((channels, 2 * width)),
            resident((channels, width)),
            resident((width, channels)),
            resident((channels, 3 * width)),
            bf16((16, 128)),
        ),
        in_hbm(
            key_weight,
            value_weight,
            query_weight,
            out_weight,
            motion_query,
            motion_key,
            motion_value,
        ),
        in_specs=[hbm] * 7,
        out_specs=(vmem,) * 4 + (whole(bf16((16, 128))),),
        scratch=[pltpu.SemaphoreType.DMA((7,))],
        moved=11500000,
    )
    tokens = call(
        tokens_kernel,
        bf16((places, channels)),
        (own, *from_z, flag),
        scratch=[pltpu.VMEM((places, channels), jnp.float32)],
        moved=700000,
    )
    from_y, tokens = lax.optimization_barrier((from_y, tokens))
    from_yc = send(from_y, C_FLIP)
    tokens_y = send(tokens, Y_FLIP)
    tokens_c = send(tokens, C_FLIP)

    args = (lat, from_c, from_y, from_yc, gain) + in_vmem(wkv, wq)
    own_parts = call(
        own_kernel,
        (
            bf16((2 * places, width)),
            f32((HEADS, 2 * places, 256)),
            f32((2 * places, 128)),
        ),
        args,
        in_specs=specs(args, 2),
        scratch=[
            pltpu.VMEM((8 * places, channels), jnp.bfloat16),
            pltpu.VMEM((8 * places, channels), jnp.bfloat16),
        ],
        flops=5400000000,
        moved=9000000,
    )
    tokens_y, own_parts = lax.optimization_barrier((tokens_y, own_parts))
    tokens_yc = send(tokens_y, C_FLIP)
    args = (tokens, tokens_c, tokens_y, tokens_yc, *own_parts, lat, bias, motion, codes)
    args += in_vmem(wkv, wo)
    block, packed = call(
        join_kernel,
        (bf16((2, places, channels)), bf16((8, 72, width))),
        args,
        in_specs=specs(args, 2),
        scratch=[
            pltpu.VMEM((4 * places, channels), jnp.bfloat16),
            pltpu.VMEM((4 * places, channels), jnp.bfloat16),
            pltpu.VMEM((2, 16, channels), jnp.float32),
        ],
        flops=2900000000,
        moved=8000000,
    )
    moving = exchange(packed)
    args = (moving,) + in_vmem(motion_qkv)
    rows = 320
    heads = call(
        motion_kernel,
        bf16((8, 40, width)),
        args,
        in_specs=specs(args, 1),
        scratch=[
            pltpu.VMEM((rows, channels), jnp.bfloat16),
            pltpu.VMEM((rows, 3 * width), jnp.bfloat16),
        ],
        flops=2200000000,
        moved=8000000,
    )
    returned = exchange(heads)
    motion_heads = call(
        place_kernel,
        bf16((2, places, width)),
        (returned,),
        scratch=[pltpu.VMEM((2, 16, width), jnp.float32)],
        moved=800000,
    )
    return (
        block.reshape(frames, row_count, col_count, channels),
        motion_heads.reshape(frames, row_count, col_count, width),
    )


def solution(mesh):
    return jax.shard_map(
        body,
        mesh=mesh,
        in_specs=(P("tm", "rows", None, None), P(("tm", "rows"), None)) + (P(),) * 10,
        out_specs=(P("tm", "rows", None, None), P("tm", "rows", None, None)),
        check_vma=False,
    )
```
